512 devices in a mesh: row: 32 (over z, core), col: 16 (over x, y).
Axes of the slice: x: 4, y: 4, z: 16, core: 2. Of those that a mesh axis runs over, the one named last changes fastest.
Arguments:
- stiff_tiles: bfloat16 [32, 16, 32, 128, 128], P('row', 'col'), may hold values from -3.5 to 3.5
- stiff_rows: int32 [32, 16, 32], P('row', 'col'), may hold values from 0 to 15, as said below
- stiff_cols: int32 [32, 16, 32], P('row', 'col'), may hold values from 0 to 31, as said below
- product_slot: int32 [32, 16, 32, 3], P('row', 'col'), may hold values from 0 to 7
- prolong_tiles: bfloat16 [512, 3, 128, 128], P(('row', 'col')), may hold values from -0.3125 to 0.3125
- coarse_dest: int32 [512, 3, 8], P(('row', 'col')), may hold values from 0 to 1023, as said below
Outputs:
- galerkin_ap: bfloat16 [512, 8, 128, 128], P(('row', 'col'))
- coarse_tiles: float32 [1024, 128, 128], P(('row', 'col'))
The draws below stay inside these ranges and needn't reach their ends.
Inputs may be any that keep to these rules, and one draw needn't show every extreme that they name: `stiff_rows`: with stiff_cols: no two entries of one device name the same row and column. Each device holds exactly 2 entries u with u = o, for every o below 16. `stiff_cols`: with stiff_rows: no two entries of one device name the same row and column. `coarse_dest`: coarse tile q is owned by device q // 2 in the order r * 16 + c; every entry held by a device names a tile owned by a device with the same index along row. The entries held by one device name the tiles of one owner at most 4 times; in each grid row some owner is named exactly 4 times by every device of that row.
All inputs are finite; a program needn't handle non-finite values.
Results may differ from the reference program's by a relative error of at most 0.017.
Values may be sent and summed in bfloat16 or wider, within the bound.
No kernel may reach another device: no remote copies, remote signals or barrier semaphores. Data moves between devices by JAX's collectives and lax.ppermute only.
A program may use at most 64 MiB of HBM per device.

```python
import jax
import jax.numpy as jnp
from jax import lax

TILE = 128
BLK = 1
KP = 3
KAP = 8
CTD = 2
MESH_ROWS = 32
MESH_COLS = 16
KA = 32
QPO = 2
ROW_BAND = 16
COL_BAND = 32
FB = 512
NCT = 1024
CONTRIB = 24
CAP = 4
N_ROW = 32
N_COL = 16


def stiff_cells(key):
    key = jax.random.fold_in(key, 5)
    device_keys = jax.random.split(key, MESH_ROWS * MESH_COLS)
    band_cells = BLK * COL_BAND

    def one_device(device_key):
        owner_keys = jax.random.split(device_key, MESH_COLS + 1)

        def one_owner(owner_key):
            return jax.random.permutation(owner_key, band_cells)[:QPO]
        picked = jax.vmap(one_owner)(owner_keys[:MESH_COLS])
        cells = (picked + (jnp.arange(MESH_COLS) * band_cells)[:, None]).reshape(-1)
        return jax.random.permutation(owner_keys[MESH_COLS], cells)
    cells = jax.vmap(one_device)(device_keys)
    return cells.reshape(MESH_ROWS, MESH_COLS, KA).astype(jnp.int32)


def draw_stiff_rows(key, part):
    cells = stiff_cells(key)
    return (cells // COL_BAND).astype(jnp.int32)


def draw_stiff_cols(key, part):
    cells = stiff_cells(key)
    return (cells % COL_BAND).astype(jnp.int32)


def draw_coarse_dest(key, part):
    key = jax.random.fold_in(key, 7)
    first_key, second_key, third_key, fourth_key = jax.random.split(key, 4)
    device_total = MESH_ROWS * MESH_COLS
    busy_owner = jax.random.randint(first_key, (MESH_ROWS,), 0, MESH_COLS).astype(jnp.int32)
    device_row = (jnp.arange(device_total) // MESH_COLS).astype(jnp.int32)
    busy_device = busy_owner[device_row]
    spare = (jnp.arange((MESH_COLS - 1) * CAP) // CAP).astype(jnp.int32)

    def others(device_key):
        return jax.random.permutation(device_key, spare)[:CONTRIB - CAP]
    chosen = jax.vmap(others)(jax.random.split(second_key, device_total))
    chosen = chosen + (chosen >= busy_device[:, None]).astype(jnp.int32)
    owners = jnp.concatenate([jnp.broadcast_to(busy_device[:, None], (device_total, CAP)), chosen], axis=1)

    def shuffle(device_key, owner_list):
        return jax.random.permutation(device_key, owner_list)
    owners = jax.vmap(shuffle)(jax.random.split(third_key, device_total), owners)
    local_tile = jax.random.randint(fourth_key, (device_total, CONTRIB), 0, CTD).astype(jnp.int32)
    destination = (device_row[:, None] * MESH_COLS + owners) * CTD + local_tile
    return destination.reshape(FB, KP, KAP).astype(jnp.int32)


def with_ends(values, rng, least, high):
    longest = values.shape.index(max(values.shape))
    spots = []
    for shift in (0, 1):
        where = [jax.random.randint(jax.random.fold_in(rng, axis), (), 0, length) for axis, length in enumerate(values.shape)]
        where[longest] = (where[longest] + shift) % values.shape[longest]
        spots.append(tuple(where))
    return values.at[spots[0]].set(least).at[spots[1]].set(high)


def block_scale(key, shape, cuts, low, high):
    factor_of, own = 1.0, jax.random.fold_in(key, 6)
    for position, shards_of in cuts:
        heights = jnp.exp(jax.random.uniform(jax.random.fold_in(own, position), (shards_of,), jnp.float32, low / len(cuts), high / len(cuts)))
        factor_of = factor_of * jnp.repeat(heights, shape[position] // shards_of).reshape([-1 if axis == position else 1 for axis in range(len(shape))])
    return factor_of


def bell_draw(rng, shape, width, bound, cuts=(), dtype=jnp.bfloat16):
    result = jax.random.normal(rng, shape, jnp.float32) * width
    if len(cuts) > 0:
        result = block_scale(rng, shape, cuts, -0.22, 0.18) * result
    return jnp.clip(result, min=-bound, max=bound).astype(dtype)


def setup_inputs(seed: int = 0) -> dict:
    seeds = jax.random.split(jax.random.key(seed), 7)
    return {
        "stiff_tiles": bell_draw(seeds[0], (MESH_ROWS, MESH_COLS, KA, TILE, TILE), (max(1, KA * KP * TILE // (KAP * BLK * 400))) ** -0.5, 3.5, ((0, 32), (1, 16))),
        "stiff_rows": draw_stiff_rows(jax.random.fold_in(seeds[6], 71), 0),
        "stiff_cols": draw_stiff_cols(jax.random.fold_in(seeds[6], 71), 0),
        "product_slot": with_ends(jax.random.randint(seeds[3], (MESH_ROWS, MESH_COLS, KA, KP), 0, KAP), jax.random.fold_in(seeds[3], 1), 0, KAP - 1).astype(jnp.int32),
        "prolong_tiles": bell_draw(seeds[4], (FB, KP, TILE, TILE), 400 ** -0.5, 0.3125, ((0, 512),)),
        "coarse_dest": draw_coarse_dest(jax.random.fold_in(seeds[6], 71), 0),
    }


def device_partial(tile_set, tile_rows, tile_cols, tile_slots, panel_rows):
    picked = jnp.take(panel_rows, tile_cols, axis=0)
    products = jnp.einsum("tij,tkjl->tkil", tile_set.astype(jnp.float32), picked.astype(jnp.float32), precision=lax.Precision.HIGHEST)
    target = (tile_rows[:, None] * KAP + tile_slots).reshape(-1)
    return jax.ops.segment_sum(products.reshape(-1, TILE, TILE), target, num_segments=ROW_BAND * KAP)


def reference(stiff_tiles, stiff_rows, stiff_cols, product_slot, prolong_tiles, coarse_dest):
    prolong_grid = prolong_tiles.reshape(N_ROW, N_COL, BLK, KP, TILE, TILE)

    def mesh_row(row_index):
        def add_device(total, col_index):
            panel_rows = prolong_grid[:, col_index].reshape(N_ROW * BLK, KP, TILE, TILE)
            partial_value = device_partial(stiff_tiles[row_index, col_index], stiff_rows[row_index, col_index], stiff_cols[row_index, col_index], product_slot[row_index, col_index], panel_rows)
            rounded = lax.optimization_barrier(partial_value.astype(jnp.bfloat16)).astype(jnp.float32)
            return total + rounded, None

        begin = jnp.zeros((ROW_BAND * KAP, TILE, TILE), jnp.float32)
        total, unused = lax.scan(add_device, begin, jnp.arange(N_COL))
        return total.astype(jnp.bfloat16)

    galerkin_ap = lax.map(mesh_row, jnp.arange(N_ROW)).reshape(FB, KAP, TILE, TILE)

    def add_band(total, row_index):
        first = (row_index * ROW_BAND).astype(jnp.int32)
        prolong_band = lax.dynamic_slice_in_dim(prolong_tiles, first, ROW_BAND, 0)
        product_band = lax.dynamic_slice_in_dim(galerkin_ap, first, ROW_BAND, 0)
        dest_band = lax.dynamic_slice_in_dim(coarse_dest, first, ROW_BAND, 0)
        pieces = jnp.einsum("gkji,gsjl->gksil", prolong_band.astype(jnp.float32), product_band.astype(jnp.float32), precision=lax.Precision.HIGHEST)
        total = total + jax.ops.segment_sum(pieces.reshape(-1, TILE, TILE), dest_band.reshape(-1), num_segments=NCT)
        return total, None

    coarse_tiles, unused = lax.scan(add_band, jnp.zeros((NCT, TILE, TILE), jnp.float32), jnp.arange(N_ROW))
    return galerkin_ap, coarse_tiles
```

```python
import jax
import jax.numpy as jnp
from jax import lax
from jax.experimental import pallas as pl
from jax.experimental.pallas import tpu as pltpu
from jax.sharding import PartitionSpec as P

TILE = 128
KP = 3
KAP = 8
CTD = 2
COLS = 16
RINGS = 16
ROWS = 2 * RINGS
KA = 32
PAIR = KA // COLS
SHARD = KP * TILE
BODY = PAIR * SHARD
MARK = 16
BLOCK = BODY + MARK
COARSE = COLS * CTD


def product_kernel(
    place_ref, row_ref, slot_ref, tile_ref, *rest
):
    pieces = rest[: len(PIECES)]
    out_ref, panel, marks, count, sems = rest[len(PIECES) :]
    copies = []
    for number, (piece, (first, size)) in enumerate(zip(pieces, PIECES)):
        for k in range(KP):
            copies.append(
                pltpu.make_async_copy(
                    piece.at[:, k],
                    panel.at[pl.ds(first, size), :, pl.ds(k * TILE, TILE)],
                    sems.at[number * KP + k],
                )
            )
    for copy in copies:
        copy.start()
    for owner in range(COLS):
        count[owner] = 0
    marks[...] = jnp.zeros_like(marks)
    lane = lax.broadcasted_iota(jnp.int32, (MARK, TILE), 1)
    for copy in copies:
        copy.wait()
    for t in range(KA):
        owner = row_ref[t]
        which = count[owner]
        count[owner] = which + 1
        product = jnp.dot(
            tile_ref[t], panel[place_ref[t]], preferred_element_type=jnp.float32
        ).astype(jnp.bfloat16)
        for k in range(KP):
            start = pl.multiple_of(which * SHARD + k * TILE, TILE)
            out_ref[owner, pl.ds(start, TILE), :] = product[:, k * TILE : (k + 1) * TILE]
        mark = jnp.zeros((MARK, TILE), jnp.float32)
        for k in range(KP):
            value = slot_ref[t * KP + k].astype(jnp.float32)
            mark = jnp.where(lane == which * KP + k, value, mark)
        marks[owner] = marks[owner] + mark
    out_ref[:, BODY:, :] = marks[...].astype(jnp.bfloat16)


def coarse_kernel(
    bucket_ref, prolong_ref, got_ref, ap_ref, out_ref,
    held, mark_held, mark_int, mark_scalar, total, merged, sems, mark_sems,
):
    chunk_total = held.shape[0]
    chunk = COLS // chunk_total
    mark_copy = pltpu.make_async_copy(got_ref.at[:, pl.ds(BODY, MARK), :], mark_held, mark_sems.at[0])
    mark_copy.start()
    copies = [
        pltpu.make_async_copy(
            got_ref.at[pl.ds(index * chunk, chunk), pl.ds(0, BODY), :], held.at[index], sems.at[index]
        )
        for index in range(chunk_total)
    ]
    for copy in copies:
        copy.start()
    mark_copy.wait()
    mark_int[...] = mark_held[...].astype(jnp.float32)[:, 0, :].astype(jnp.int32)
    scalar_copy = pltpu.make_async_copy(mark_int, mark_scalar, mark_sems.at[1])
    scalar_copy.start()
    total[...] = jnp.zeros_like(total)
    merged[...] = jnp.zeros_like(merged)
    scalar_copy.wait()
    for index in range(chunk_total):
        copies[index].wait()
        for peer in range(chunk):
            for q in range(PAIR * KP):
                slot = mark_scalar[index * chunk + peer, q]
                total[slot] = total[slot] + held[index, peer, pl.ds(q * TILE, TILE), :].astype(jnp.float32)
    for s in range(KAP):
        ap = total[s].astype(jnp.bfloat16)
        ap_ref[s] = ap
        for k in range(KP):
            term = lax.dot_general(
                prolong_ref[k], ap, (((0,), (0,)), ((), ())), preferred_element_type=jnp.float32
            )
            bucket = bucket_ref[k * KAP + s]
            merged[bucket] = merged[bucket] + term
    out_ref[...] = merged[...].astype(jnp.bfloat16)


PIECES = ((0, 4), (4, 4), (8, 4), (12, 2), (14, 2), (16, 4), (20, 4), (24, 4), (28, 2), (30, 2))


def shifted(array, step):
    pairs = [
        (2 * z + core, 2 * ((z + step) % RINGS) + core) for z in range(RINGS) for core in range(2)
    ]
    return lax.ppermute(array, "row", pairs)


def to_sibling(array):
    return lax.ppermute(array, "row", [(r, r ^ 1) for r in range(ROWS)])


def gather_pieces(prolong):
    own = prolong.reshape(SHARD, TILE)
    half = SHARD // 2
    below = shifted(own, 4)
    above = shifted(own, -4)
    first = shifted(above[:half], -4)
    second = shifted(below[half:], 4)
    own4 = jnp.concatenate([own, below, first, second, above])
    prev4 = shifted(own4, 1)
    next4 = shifted(own4, -1)
    far_next = shifted(next4[: 2 * SHARD], -1)
    far_prev = shifted(prev4[SHARD : 3 * SHARD], 1)
    mine = [own4, prev4, next4, far_next, far_prev]
    pieces = mine + [to_sibling(piece) for piece in mine]
    return [piece.reshape(-1, KP, TILE, TILE) for piece in pieces]


def panel_place(tile_cols):
    row = lax.axis_index("row")
    delta = (tile_cols // 2 - row // 2) % RINGS
    kind = delta % 4
    base = jnp.where(kind == 0, 0, jnp.where(kind == 3, 4, jnp.where(kind == 1, 8, 12)))
    offset = jnp.where(kind == 3, -1, kind)
    index = ((offset - delta + 2 * RINGS) // 4) % 4
    return base + index + jnp.where(tile_cols % 2 == row % 2, 0, RINGS)


def on_device(stiff_tiles, stiff_rows, stiff_cols, product_slot, prolong_tiles, coarse_dest):
    scalars = pl.BlockSpec(memory_space=pltpu.SMEM)
    vmem = pl.BlockSpec(memory_space=pltpu.VMEM)
    anywhere = pl.BlockSpec(memory_space=pl.ANY)
    prolong = prolong_tiles[0]
    pieces = gather_pieces(prolong)
    place = panel_place(stiff_cols[0, 0])
    sent = pl.pallas_call(
        product_kernel,
        out_shape=jax.ShapeDtypeStruct((COLS, BLOCK, TILE), jnp.bfloat16),
        in_specs=[scalars] * 3 + [vmem] + [anywhere] * len(PIECES),
        out_specs=vmem,
        scratch_shapes=[
            pltpu.VMEM((ROWS, TILE, SHARD), jnp.bfloat16),
            pltpu.VMEM((COLS, MARK, TILE), jnp.float32),
            pltpu.SMEM((COLS,), jnp.int32),
            pltpu.SemaphoreType.DMA((len(PIECES) * KP,)),
        ],
        compiler_params=pltpu.CompilerParams(vmem_limit_bytes=24 * 2**20),
    )(place, stiff_rows[0, 0], product_slot[0, 0].reshape(KA * KP), stiff_tiles[0, 0], *pieces)
    got = lax.all_to_all(sent, "col", split_axis=0, concat_axis=0, tiled=True)
    chunk_total = 4
    ap, merged = pl.pallas_call(
        coarse_kernel,
        out_shape=(
            jax.ShapeDtypeStruct((KAP, TILE, TILE), jnp.bfloat16),
            jax.ShapeDtypeStruct((COARSE, TILE, TILE), jnp.bfloat16),
        ),
        in_specs=[scalars, vmem, anywhere],
        out_specs=(vmem, vmem),
        scratch_shapes=[
            pltpu.VMEM((chunk_total, COLS // chunk_total, BODY, TILE), jnp.bfloat16),
            pltpu.VMEM((COLS, MARK, TILE), jnp.bfloat16),
            pltpu.VMEM((COLS, TILE), jnp.int32),
            pltpu.SMEM((COLS, TILE), jnp.int32),
            pltpu.VMEM((KAP, TILE, TILE), jnp.float32),
            pltpu.VMEM((COARSE, TILE, TILE), jnp.float32),
            pltpu.SemaphoreType.DMA((chunk_total,)),
            pltpu.SemaphoreType.DMA((2,)),
        ],
        compiler_params=pltpu.CompilerParams(vmem_limit_bytes=24 * 2**20),
    )(coarse_dest.reshape(KP * KAP) % COARSE, prolong, got)
    received = lax.all_to_all(merged, "col", split_axis=0, concat_axis=0, tiled=True)
    coarse = jnp.sum(received.reshape(COLS, CTD, TILE, TILE).astype(jnp.float32), axis=0)
    return (ap[None], coarse)


def solution(mesh):
    in_specs = (
        P("row", "col", None, None, None),
        P("row", "col", None),
        P("row", "col", None),
        P("row", "col", None, None),
        P(("row", "col"), None, None, None),
        P(("row", "col"), None, None),
    )
    out_specs = (P(("row", "col"), None, None, None), P(("row", "col"), None, None))
    return jax.shard_map(
        on_device, mesh=mesh, in_specs=in_specs, out_specs=out_specs, check_vma=False
    )
```

```python
import jax
import jax.numpy as jnp
from jax import lax
from jax.experimental import pallas as pl
from jax.experimental.pallas import tpu as pltpu
from jax.sharding import PartitionSpec as P

TILE = 128
KP = 3
KAP = 8
CTD = 2
COLS = 16
RINGS = 16
ROWS = 2 * RINGS
KA = 32
PAIR = KA // COLS
SHARD = KP * TILE
BODY = PAIR * SHARD
MARK = 16
BLOCK = BODY + MARK
COARSE = COLS * CTD
K1_MIB = 57
SPOT = 2 * KA + KA * KP


def product_kernel(scalar_ref, tile_ref, *rest):
    pieces = rest[: len(PIECES)]
    out_ref, panel, tiles, outs, order, count, sems, tile_sem, out_sems = rest[len(PIECES) :]
    tile_copy = pltpu.make_async_copy(tile_ref, tiles, tile_sem.at[0])
    tile_copy.start()
    copies = []
    for number, (piece, (first, size)) in enumerate(zip(pieces, PIECES)):
        for k in range(KP):
            copies.append(
                pltpu.make_async_copy(
                    piece.at[:, k],
                    panel.at[pl.ds(first, size), :, pl.ds(k * TILE, TILE)],
                    sems.at[number * KP + k],
                )
            )
    for copy in copies:
        copy.start()
    for owner in range(COLS):
        count[owner] = 0
    for t in range(KA):
        owner = scalar_ref[KA + t]
        which = count[owner]
        count[owner] = which + 1
        order[owner * PAIR + which] = t
    lane = lax.broadcasted_iota(jnp.int32, (MARK, TILE), 1)
    tile_copy.wait()
    for copy in copies:
        copy.wait()
    out_copies = []
    for owner in range(COLS):
        mark = jnp.zeros((MARK, TILE), jnp.float32)
        for which in range(PAIR):
            t = order[owner * PAIR + which]
            product = jnp.dot(
                tiles[t], panel[scalar_ref[t]], preferred_element_type=jnp.float32
            ).astype(jnp.bfloat16)
            for k in range(KP):
                q = which * KP + k
                outs[owner, q * TILE : (q + 1) * TILE, :] = product[:, k * TILE : (k + 1) * TILE]
                value = scalar_ref[2 * KA + t * KP + k].astype(jnp.float32)
                mark = jnp.where(lane == q, value, mark)
        outs[owner, BODY:, :] = mark.astype(jnp.bfloat16)
        out_copy = pltpu.make_async_copy(outs.at[owner], out_ref.at[owner], out_sems.at[owner])
        out_copy.start()
        out_copies.append(out_copy)
    for out_copy in out_copies:
        out_copy.wait()


def coarse_kernel(
    scalar_ref, prolong_ref, got_ref, ap_ref, out_ref,
    held, mark_held, mark_int, mark_scalar, total, merged, rounded, sems, mark_sems,
):
    chunk_total = held.shape[0]
    chunk = COLS // chunk_total
    mark_copy = pltpu.make_async_copy(got_ref.at[:, pl.ds(BODY, MARK), :], mark_held, mark_sems.at[0])
    mark_copy.start()
    copies = [
        pltpu.make_async_copy(
            got_ref.at[pl.ds(index * chunk, chunk), pl.ds(0, BODY), :], held.at[index], sems.at[index]
        )
        for index in range(chunk_total)
    ]
    for copy in copies:
        copy.start()
    mark_copy.wait()
    mark_int[...] = mark_held[...].astype(jnp.float32)[:, 0, :].astype(jnp.int32)
    scalar_copy = pltpu.make_async_copy(mark_int, mark_scalar, mark_sems.at[1])
    scalar_copy.start()
    total[...] = jnp.zeros_like(total)
    merged[...] = jnp.zeros_like(merged)
    scalar_copy.wait()
    for index in range(chunk_total):
        copies[index].wait()
        for peer in range(chunk):
            for q in range(PAIR * KP):
                slot = mark_scalar[index * chunk + peer, q]
                total[slot] = total[slot] + held[index, peer, pl.ds(q * TILE, TILE), :].astype(jnp.float32)
    for s in range(KAP):
        ap = total[s].astype(jnp.bfloat16)
        ap_ref[s] = ap
        for k in range(KP):
            term = lax.dot_general(
                prolong_ref[k], ap, (((0,), (0,)), ((), ())), preferred_element_type=jnp.float32
            )
            bucket = scalar_ref[SPOT + k * KAP + s]
            merged[bucket] = merged[bucket] + term
    rounded[...] = merged[...].astype(jnp.bfloat16)
    out_copy = pltpu.make_async_copy(rounded, out_ref, mark_sems.at[2])
    out_copy.start()
    out_copy.wait()


PIECES = ((0, 8), (8, 4), (12, 4), (16, 8), (24, 4), (28, 4))


def shifted(array, step):
    pairs = [
        (2 * z + core, 2 * ((z + step) % RINGS) + core) for z in range(RINGS) for core in range(2)
    ]
    return lax.ppermute(array, "row", pairs)


def to_sibling(array):
    return lax.ppermute(array, "row", [(r, r ^ 1) for r in range(ROWS)])


def gather_pieces(prolong, numbers):
    groups = [[2 * (low + 2 * k) + core for k in range(8)] for low in range(2) for core in range(2)]
    own8 = lax.all_gather(
        prolong.reshape(SHARD, TILE), "row", axis=0, tiled=True, axis_index_groups=groups
    )
    other8 = to_sibling(own8)
    low4 = shifted(own8[: 4 * SHARD], 1)
    high4 = shifted(own8[4 * SHARD :], -1)
    low4, high4, numbers = lax.optimization_barrier((low4, high4, numbers))
    pieces = [own8, low4, high4, other8, to_sibling(low4), to_sibling(high4)]
    return [piece.reshape(-1, KP, TILE, TILE) for piece in pieces], numbers


def panel_place(tile_cols):
    row = lax.axis_index("row")
    ring = tile_cols // 2
    return (
        ring // 2
        + jnp.where((ring - row // 2) % 2 == 0, 0, 8)
        + jnp.where((tile_cols - row) % 2 == 0, 0, RINGS)
    )


def on_device(stiff_tiles, stiff_rows, stiff_cols, product_slot, prolong_tiles, coarse_dest):
    scalars = pl.BlockSpec(memory_space=pltpu.SMEM)
    vmem = pl.BlockSpec(memory_space=pltpu.VMEM)
    hbm = pl.BlockSpec(memory_space=pltpu.HBM)
    anywhere = pl.BlockSpec(memory_space=pl.ANY)
    params = pltpu.CompilerParams(vmem_limit_bytes=24 * 2**20)
    prolong = prolong_tiles[0]
    numbers = jnp.concatenate(
        [
            panel_place(stiff_cols[0, 0]),
            stiff_rows[0, 0],
            product_slot[0, 0].reshape(KA * KP),
            coarse_dest.reshape(KP * KAP) % COARSE,
        ]
    )
    pieces, numbers = gather_pieces(prolong, numbers)
    sent = pl.pallas_call(
        product_kernel,
        out_shape=jax.ShapeDtypeStruct((COLS, BLOCK, TILE), jnp.bfloat16),
        in_specs=[scalars, hbm] + [anywhere] * len(PIECES),
        out_specs=hbm,
        scratch_shapes=[
            pltpu.VMEM((ROWS, TILE, SHARD), jnp.bfloat16),
            pltpu.VMEM((KA, TILE, TILE), jnp.bfloat16),
            pltpu.VMEM((COLS, BLOCK, TILE), jnp.bfloat16),
            pltpu.SMEM((KA,), jnp.int32),
            pltpu.SMEM((COLS,), jnp.int32),
            pltpu.SemaphoreType.DMA((len(PIECES) * KP,)),
            pltpu.SemaphoreType.DMA((1,)),
            pltpu.SemaphoreType.DMA((COLS,)),
        ],
        compiler_params=pltpu.CompilerParams(vmem_limit_bytes=K1_MIB * 2**20),
    )(numbers, stiff_tiles[0, 0], *pieces)
    got = lax.all_to_all(sent, "col", split_axis=0, concat_axis=0, tiled=True)
    chunk_total = 4
    ap, merged = pl.pallas_call(
        coarse_kernel,
        out_shape=(
            jax.ShapeDtypeStruct((KAP, TILE, TILE), jnp.bfloat16),
            jax.ShapeDtypeStruct((COARSE, TILE, TILE), jnp.bfloat16),
        ),
        in_specs=[scalars, vmem, hbm],
        out_specs=(vmem, hbm),
        scratch_shapes=[
            pltpu.VMEM((chunk_total, COLS // chunk_total, BODY, TILE), jnp.bfloat16),
            pltpu.VMEM((COLS, MARK, TILE), jnp.bfloat16),
            pltpu.VMEM((COLS, TILE), jnp.int32),
            pltpu.SMEM((COLS, TILE), jnp.int32),
            pltpu.VMEM((KAP, TILE, TILE), jnp.float32),
            pltpu.VMEM((COARSE, TILE, TILE), jnp.float32),
            pltpu.VMEM((COARSE, TILE, TILE), jnp.bfloat16),
            pltpu.SemaphoreType.DMA((chunk_total,)),
            pltpu.SemaphoreType.DMA((3,)),
        ],
        compiler_params=params,
    )(numbers, prolong, got)
    received = lax.all_to_all(merged, "col", split_axis=0, concat_axis=0, tiled=True)
    coarse = jnp.sum(received.reshape(COLS, CTD, TILE, TILE).astype(jnp.float32), axis=0)
    return (ap[None], coarse)


def solution(mesh):
    in_specs = (
        P("row", "col", None, None, None),
        P("row", "col", None),
        P("row", "col", None),
        P("row", "col", None, None),
        P(("row", "col"), None, None, None),
        P(("row", "col"), None, None),
    )
    out_specs = (P(("row", "col"), None, None, None), P(("row", "col"), None, None))
    return jax.shard_map(
        on_device, mesh=mesh, in_specs=in_specs, out_specs=out_specs, check_vma=False
    )
```

```python
import jax
import jax.numpy as jnp
from jax import lax
from jax.experimental import pallas as pl
from jax.experimental.pallas import tpu as pltpu
from jax.sharding import PartitionSpec as P

TILE = 128
KP = 3
KAP = 8
CTD = 2
COLS = 16
RINGS = 16
ROWS = 2 * RINGS
KA = 32
PAIR = KA // COLS
SHARD = KP * TILE
BODY = PAIR * SHARD
MARK = 16
BLOCK = BODY + MARK
COARSE = COLS * CTD
K1_MIB = 24
SPOT = 2 * KA + KA * KP


def product_kernel(scalar_ref, tile_ref, *rest):
    pieces = rest[: len(PIECES)]
    outs, panel, tiles, order, count, sems, tile_sem = rest[len(PIECES) :]
    tile_copy = pltpu.make_async_copy(tile_ref, tiles, tile_sem.at[0])
    tile_copy.start()
    copies = []
    for number, (piece, (first, size)) in enumerate(zip(pieces, PIECES)):
        for k in range(KP):
            copies.append(
                pltpu.make_async_copy(
                    piece.at[:, k],
                    panel.at[pl.ds(first, size), :, pl.ds(k * TILE, TILE)],
                    sems.at[number * KP + k],
                )
            )
    for copy in copies:
        copy.start()
    for owner in range(COLS):
        count[owner] = 0
    for t in range(KA):
        owner = scalar_ref[KA + t]
        which = count[owner]
        count[owner] = which + 1
        order[owner * PAIR + which] = t
    lane = lax.broadcasted_iota(jnp.int32, (MARK, TILE), 1)
    tile_copy.wait()
    for copy in copies:
        copy.wait()
    for owner in range(COLS):
        mark = jnp.zeros((MARK, TILE), jnp.float32)
        for which in range(PAIR):
            t = order[owner * PAIR + which]
            product = jnp.dot(
                tiles[t], panel[scalar_ref[t]], preferred_element_type=jnp.float32
            ).astype(jnp.bfloat16)
            for k in range(KP):
                q = which * KP + k
                outs[owner, q * TILE : (q + 1) * TILE, :] = product[:, k * TILE : (k + 1) * TILE]
                value = scalar_ref[2 * KA + t * KP + k].astype(jnp.float32)
                mark = jnp.where(lane == q, value, mark)
        outs[owner, BODY:, :] = mark.astype(jnp.bfloat16)


def coarse_kernel(
    scalar_ref, prolong_ref, got_ref, ap_ref, out_ref,
    held, mark_held, mark_int, mark_scalar, total, merged, rounded, sems, mark_sems,
):
    chunk_total = held.shape[0]
    chunk = COLS // chunk_total
    mark_copy = pltpu.make_async_copy(got_ref.at[:, pl.ds(BODY, MARK), :], mark_held, mark_sems.at[0])
    mark_copy.start()
    copies = [
        pltpu.make_async_copy(
            got_ref.at[pl.ds(index * chunk, chunk), pl.ds(0, BODY), :], held.at[index], sems.at[index]
        )
        for index in range(chunk_total)
    ]
    for copy in copies:
        copy.start()
    mark_copy.wait()
    mark_int[...] = mark_held[...].astype(jnp.float32)[:, 0, :].astype(jnp.int32)
    scalar_copy = pltpu.make_async_copy(mark_int, mark_scalar, mark_sems.at[1])
    scalar_copy.start()
    total[...] = jnp.zeros_like(total)
    merged[...] = jnp.zeros_like(merged)
    scalar_copy.wait()
    for index in range(chunk_total):
        copies[index].wait()
        for peer in range(chunk):
            for q in range(PAIR * KP):
                slot = mark_scalar[index * chunk + peer, q]
                total[slot] = total[slot] + held[index, peer, pl.ds(q * TILE, TILE), :].astype(jnp.float32)
    for s in range(KAP):
        ap = total[s].astype(jnp.bfloat16)
        ap_ref[s] = ap
        for k in range(KP):
            term = lax.dot_general(
                prolong_ref[k], ap, (((0,), (0,)), ((), ())), preferred_element_type=jnp.float32
            )
            bucket = scalar_ref[SPOT + k * KAP + s]
            merged[bucket] = merged[bucket] + term
    rounded[...] = merged[...].astype(jnp.bfloat16)
    out_copy = pltpu.make_async_copy(rounded, out_ref, mark_sems.at[2])
    out_copy.start()
    out_copy.wait()


PIECES = ((0, 16), (16, 16))


def from_neighbour(array):
    pairs = [
        (2 * z + core, 2 * ((z + (1 if core == 0 else -1)) % RINGS) + core)
        for z in range(RINGS)
        for core in range(2)
    ]
    return lax.ppermute(array, "row", pairs)


def to_sibling(array):
    return lax.ppermute(array, "row", [(r, r ^ 1) for r in range(ROWS)])


def gather_pieces(prolong, numbers):
    groups = [[2 * (low + 2 * k) + core for k in range(8)] for low in range(2) for core in range(2)]
    same8 = lax.all_gather(
        prolong.reshape(SHARD, TILE), "row", axis=0, tiled=True, axis_index_groups=groups
    )
    next8 = from_neighbour(same8)
    next8, numbers = lax.optimization_barrier((next8, numbers))
    own16 = jnp.concatenate([same8, next8])
    pieces = [own16, to_sibling(own16)]
    return [piece.reshape(-1, KP, TILE, TILE) for piece in pieces], numbers


def panel_place(tile_cols):
    row = lax.axis_index("row")
    ring = tile_cols // 2
    return (
        ring // 2
        + jnp.where((ring - row // 2) % 2 == 0, 0, 8)
        + jnp.where((tile_cols - row) % 2 == 0, 0, RINGS)
    )


def on_device(stiff_tiles, stiff_rows, stiff_cols, product_slot, prolong_tiles, coarse_dest):
    scalars = pl.BlockSpec(memory_space=pltpu.SMEM)
    vmem = pl.BlockSpec(memory_space=pltpu.VMEM)
    hbm = pl.BlockSpec(memory_space=pltpu.HBM)
    anywhere = pl.BlockSpec(memory_space=pl.ANY)
    params = pltpu.CompilerParams(vmem_limit_bytes=24 * 2**20)
    prolong = prolong_tiles[0]
    numbers = jnp.concatenate(
        [
            panel_place(stiff_cols[0, 0]),
            stiff_rows[0, 0],
            product_slot[0, 0].reshape(KA * KP),
            coarse_dest.reshape(KP * KAP) % COARSE,
        ]
    )
    pieces, numbers = gather_pieces(prolong, numbers)
    sent = pl.pallas_call(
        product_kernel,
        out_shape=jax.ShapeDtypeStruct((COLS, BLOCK, TILE), jnp.bfloat16),
        in_specs=[scalars, hbm] + [anywhere] * len(PIECES),
        out_specs=vmem,
        scratch_shapes=[
            pltpu.VMEM((ROWS, TILE, SHARD), jnp.bfloat16),
            pltpu.VMEM((KA, TILE, TILE), jnp.bfloat16),
            pltpu.SMEM((KA,), jnp.int32),
            pltpu.SMEM((COLS,), jnp.int32),
            pltpu.SemaphoreType.DMA((len(PIECES) * KP,)),
            pltpu.SemaphoreType.DMA((1,)),
        ],
        compiler_params=pltpu.CompilerParams(vmem_limit_bytes=K1_MIB * 2**20),
    )(numbers, stiff_tiles[0, 0], *pieces)
    got = lax.all_to_all(sent, "col", split_axis=0, concat_axis=0, tiled=True)
    chunk_total = 4
    ap, merged = pl.pallas_call(
        coarse_kernel,
        out_shape=(
            jax.ShapeDtypeStruct((KAP, TILE, TILE), jnp.bfloat16),
            jax.ShapeDtypeStruct((COARSE, TILE, TILE), jnp.bfloat16),
        ),
        in_specs=[scalars, vmem, hbm],
        out_specs=(vmem, hbm),
        scratch_shapes=[
            pltpu.VMEM((chunk_total, COLS // chunk_total, BODY, TILE), jnp.bfloat16),
            pltpu.VMEM((COLS, MARK, TILE), jnp.bfloat16),
            pltpu.VMEM((COLS, TILE), jnp.int32),
            pltpu.SMEM((COLS, TILE), jnp.int32),
            pltpu.VMEM((KAP, TILE, TILE), jnp.float32),
            pltpu.VMEM((COARSE, TILE, TILE), jnp.float32),
            pltpu.VMEM((COARSE, TILE, TILE), jnp.bfloat16),
            pltpu.SemaphoreType.DMA((chunk_total,)),
            pltpu.SemaphoreType.DMA((3,)),
        ],
        compiler_params=params,
    )(numbers, prolong, got)
    received = lax.all_to_all(merged, "col", split_axis=0, concat_axis=0, tiled=True)
    coarse = jnp.sum(received.reshape(COLS, CTD, TILE, TILE).astype(jnp.float32), axis=0)
    return (ap[None], coarse)


def solution(mesh):
    in_specs = (
        P("row", "col", None, None, None),
        P("row", "col", None),
        P("row", "col", None),
        P("row", "col", None, None),
        P(("row", "col"), None, None, None),
        P(("row", "col"), None, None),
    )
    out_specs = (P(("row", "col"), None, None, None), P(("row", "col"), None, None))
    return jax.shard_map(
        on_device, mesh=mesh, in_specs=in_specs, out_specs=out_specs, check_vma=False
    )
```

```python
import jax
import jax.numpy as jnp
from jax import lax
from jax.experimental import pallas as pl
from jax.experimental.pallas import tpu as pltpu
from jax.sharding import PartitionSpec as P

TILE = 128
KP = 3
KAP = 8
SIDE = 4
CTD = 2
COLS = 16
RINGS = 16
ROWS = 2 * RINGS
KA = 32
PAIR = KA // COLS
SHARD = KP * TILE
BODY = PAIR * SHARD
MARK = 16
BLOCK = BODY + MARK
COARSE = COLS * CTD
K1_MIB = 24
SPOT = 2 * KA + KA * KP


def product_kernel(scalar_ref, tile_ref, *rest):
    pieces = rest[: len(PIECES)]
    outs, panel, tiles, order, count, sems, tile_sem = rest[len(PIECES) :]
    tile_copy = pltpu.make_async_copy(tile_ref, tiles, tile_sem.at[0])
    tile_copy.start()
    copies = []
    for number, (piece, (first, size)) in enumerate(zip(pieces, PIECES)):
        for k in range(KP):
            copies.append(
                pltpu.make_async_copy(
                    piece.at[:, k],
                    panel.at[pl.ds(first, size), :, pl.ds(k * TILE, TILE)],
                    sems.at[number * KP + k],
                )
            )
    for copy in copies:
        copy.start()
    for owner in range(COLS):
        count[owner] = 0
    for t in range(KA):
        owner = scalar_ref[KA + t]
        which = count[owner]
        count[owner] = which + 1
        order[owner * PAIR + which] = t
    lane = lax.broadcasted_iota(jnp.int32, (MARK, TILE), 1)
    tile_copy.wait()
    for copy in copies:
        copy.wait()
    flipped = scalar_ref[SPOT + KP * KAP]
    for place in range(COLS):
        owner = jnp.where(flipped == 0, place, place % SIDE * SIDE + place // SIDE)
        mark = jnp.zeros((MARK, TILE), jnp.float32)
        for which in range(PAIR):
            t = order[owner * PAIR + which]
            product = jnp.dot(
                tiles[t], panel[scalar_ref[t]], preferred_element_type=jnp.float32
            ).astype(jnp.bfloat16)
            for k in range(KP):
                q = which * KP + k
                outs[place, q * TILE : (q + 1) * TILE, :] = product[:, k * TILE : (k + 1) * TILE]
                value = scalar_ref[2 * KA + t * KP + k].astype(jnp.float32)
                mark = jnp.where(lane == q, value, mark)
        outs[place, BODY:, :] = mark.astype(jnp.bfloat16)


def slot_kernel(got_ref, out_ref, mark_int, mark_scalar, total, sem):
    marks = got_ref[:, BODY:, :].astype(jnp.float32)
    mark_int[...] = marks[:, 0, :].astype(jnp.int32)
    scalar_copy = pltpu.make_async_copy(mark_int, mark_scalar, sem.at[0])
    scalar_copy.start()
    total[...] = jnp.zeros_like(total)
    scalar_copy.wait()
    for peer in range(SIDE):
        for owner in range(SIDE):
            block = peer * SIDE + owner
            for q in range(PAIR * KP):
                where = owner * KAP + mark_scalar[block, q]
                part = got_ref[block, q * TILE : (q + 1) * TILE, :]
                total[where] = total[where] + part.astype(jnp.float32)
    out_ref[...] = total[...].astype(jnp.bfloat16)


def coarse_kernel(scalar_ref, prolong_ref, got_ref, ap_ref, out_ref, merged):
    merged[...] = jnp.zeros_like(merged)
    for s in range(KAP):
        total = got_ref[s].astype(jnp.float32)
        for peer in range(1, SIDE):
            total = total + got_ref[peer * KAP + s].astype(jnp.float32)
        ap = total.astype(jnp.bfloat16)
        ap_ref[s] = ap
        for k in range(KP):
            term = lax.dot_general(
                prolong_ref[k], ap, (((0,), (0,)), ((), ())), preferred_element_type=jnp.float32
            )
            bucket = scalar_ref[SPOT + k * KAP + s]
            merged[bucket] = merged[bucket] + term
    out_ref[...] = merged[...].astype(jnp.bfloat16)


def side_groups(even_along_x):
    groups = []
    for row in range(ROWS):
        along_x = (row % 2 == 0) == even_along_x
        for fixed in range(SIDE):
            groups.append(
                [
                    row * COLS + (move * SIDE + fixed if along_x else fixed * SIDE + move)
                    for move in range(SIDE)
                ]
            )
    return groups


def exchange_side(array, even_along_x):
    return lax.all_to_all(
        array,
        ("row", "col"),
        split_axis=0,
        concat_axis=0,
        tiled=True,
        axis_index_groups=side_groups(even_along_x),
    )


PIECES = ((0, 16), (16, 16))


def from_neighbour(array):
    pairs = [
        (2 * z + core, 2 * ((z + (1 if core == 0 else -1)) % RINGS) + core)
        for z in range(RINGS)
        for core in range(2)
    ]
    return lax.ppermute(array, "row", pairs)


def to_sibling(array):
    return lax.ppermute(array, "row", [(r, r ^ 1) for r in range(ROWS)])


def gather_pieces(prolong, numbers):
    groups = [[2 * (low + 2 * k) + core for k in range(8)] for low in range(2) for core in range(2)]
    same8 = lax.all_gather(
        prolong.reshape(SHARD, TILE), "row", axis=0, tiled=True, axis_index_groups=groups
    )
    next8 = from_neighbour(same8)
    next8, numbers = lax.optimization_barrier((next8, numbers))
    own16 = jnp.concatenate([same8, next8])
    pieces = [own16, to_sibling(own16)]
    return [piece.reshape(-1, KP, TILE, TILE) for piece in pieces], numbers


def panel_place(tile_cols):
    row = lax.axis_index("row")
    ring = tile_cols // 2
    return (
        ring // 2
        + jnp.where((ring - row // 2) % 2 == 0, 0, 8)
        + jnp.where((tile_cols - row) % 2 == 0, 0, RINGS)
    )


def on_device(stiff_tiles, stiff_rows, stiff_cols, product_slot, prolong_tiles, coarse_dest):
    scalars = pl.BlockSpec(memory_space=pltpu.SMEM)
    vmem = pl.BlockSpec(memory_space=pltpu.VMEM)
    hbm = pl.BlockSpec(memory_space=pltpu.HBM)
    anywhere = pl.BlockSpec(memory_space=pl.ANY)
    params = pltpu.CompilerParams(vmem_limit_bytes=24 * 2**20)
    prolong = prolong_tiles[0]
    numbers = jnp.concatenate(
        [
            panel_place(stiff_cols[0, 0]),
            stiff_rows[0, 0],
            product_slot[0, 0].reshape(KA * KP),
            coarse_dest.reshape(KP * KAP) % COARSE,
            jnp.full((1,), lax.axis_index("row") % 2, jnp.int32),
        ]
    )
    pieces, numbers = gather_pieces(prolong, numbers)
    sent = pl.pallas_call(
        product_kernel,
        out_shape=jax.ShapeDtypeStruct((COLS, BLOCK, TILE), jnp.bfloat16),
        in_specs=[scalars, hbm] + [anywhere] * len(PIECES),
        out_specs=vmem,
        scratch_shapes=[
            pltpu.VMEM((ROWS, TILE, SHARD), jnp.bfloat16),
            pltpu.VMEM((KA, TILE, TILE), jnp.bfloat16),
            pltpu.SMEM((KA,), jnp.int32),
            pltpu.SMEM((COLS,), jnp.int32),
            pltpu.SemaphoreType.DMA((len(PIECES) * KP,)),
            pltpu.SemaphoreType.DMA((1,)),
        ],
        compiler_params=pltpu.CompilerParams(vmem_limit_bytes=K1_MIB * 2**20),
    )(numbers, stiff_tiles[0, 0], *pieces)
    got = exchange_side(sent, True)
    partial = pl.pallas_call(
        slot_kernel,
        out_shape=jax.ShapeDtypeStruct((SIDE * KAP, TILE, TILE), jnp.bfloat16),
        in_specs=[vmem],
        out_specs=vmem,
        scratch_shapes=[
            pltpu.VMEM((COLS, TILE), jnp.int32),
            pltpu.SMEM((COLS, TILE), jnp.int32),
            pltpu.VMEM((SIDE * KAP, TILE, TILE), jnp.float32),
            pltpu.SemaphoreType.DMA((1,)),
        ],
        compiler_params=params,
    )(got)
    summed = exchange_side(partial, False)
    ap, merged = pl.pallas_call(
        coarse_kernel,
        out_shape=(
            jax.ShapeDtypeStruct((KAP, TILE, TILE), jnp.bfloat16),
            jax.ShapeDtypeStruct((COARSE, TILE, TILE), jnp.bfloat16),
        ),
        in_specs=[scalars, vmem, vmem],
        out_specs=(vmem, vmem),
        scratch_shapes=[pltpu.VMEM((COARSE, TILE, TILE), jnp.float32)],
        compiler_params=params,
    )(numbers, prolong, summed)
    received = lax.all_to_all(merged, "col", split_axis=0, concat_axis=0, tiled=True)
    coarse = jnp.sum(received.reshape(COLS, CTD, TILE, TILE).astype(jnp.float32), axis=0)
    return (ap[None], coarse)


def solution(mesh):
    in_specs = (
        P("row", "col", None, None, None),
        P("row", "col", None),
        P("row", "col", None),
        P("row", "col", None, None),
        P(("row", "col"), None, None, None),
        P(("row", "col"), None, None),
    )
    out_specs = (P(("row", "col"), None, None, None), P(("row", "col"), None, None))
    return jax.shard_map(
        on_device, mesh=mesh, in_specs=in_specs, out_specs=out_specs, check_vma=False
    )
```

```python
import jax
import jax.numpy as jnp
from jax import lax
from jax.experimental import pallas as pl
from jax.experimental.pallas import tpu as pltpu
from jax.sharding import PartitionSpec as P

TILE = 128
KP = 3
KAP = 8
SIDE = 4
CTD = 2
COLS = 16
RINGS = 16
ROWS = 2 * RINGS
KA = 32
PAIR = KA // COLS
SHARD = KP * TILE
BODY = PAIR * SHARD
MARK = 16
BLOCK = BODY + MARK
COARSE = COLS * CTD
K1_MIB = 24
SPOT = 2 * KA + KA * KP


def product_kernel(scalar_ref, tile_ref, own_ref, other_ref, outs, order, count):
    for owner in range(COLS):
        count[owner] = 0
    for t in range(KA):
        owner = scalar_ref[KA + t]
        which = count[owner]
        count[owner] = which + 1
        order[owner * PAIR + which] = t
    lane = lax.broadcasted_iota(jnp.int32, (MARK, TILE), 1)
    flipped = scalar_ref[SPOT + KP * KAP]
    for place in range(COLS):
        owner = jnp.where(flipped == 0, place, place % SIDE * SIDE + place // SIDE)
        mark = jnp.zeros((MARK, TILE), jnp.float32)
        for which in range(PAIR):
            t = order[owner * PAIR + which]
            spot = scalar_ref[t]
            mine = spot < RINGS
            shard = spot % RINGS
            tile = tile_ref[t]
            for k in range(KP):
                q = which * KP + k
                block = jnp.where(mine, own_ref[shard, k], other_ref[shard, k])
                product = jnp.dot(tile, block, preferred_element_type=jnp.float32)
                outs[place, q * TILE : (q + 1) * TILE, :] = product.astype(jnp.bfloat16)
                value = scalar_ref[2 * KA + t * KP + k].astype(jnp.float32)
                mark = jnp.where(lane == q, value, mark)
        outs[place, BODY:, :] = mark.astype(jnp.bfloat16)


def slot_kernel(got_ref, out_ref, mark_int, mark_scalar, total, sem):
    marks = got_ref[:, BODY:, :].astype(jnp.float32)
    mark_int[...] = marks[:, 0, :].astype(jnp.int32)
    scalar_copy = pltpu.make_async_copy(mark_int, mark_scalar, sem.at[0])
    scalar_copy.start()
    total[...] = jnp.zeros_like(total)
    scalar_copy.wait()
    for peer in range(SIDE):
        for owner in range(SIDE):
            block = peer * SIDE + owner
            for q in range(PAIR * KP):
                where = owner * KAP + mark_scalar[block, q]
                part = got_ref[block, q * TILE : (q + 1) * TILE, :]
                total[where] = total[where] + part.astype(jnp.float32)
    out_ref[...] = total[...].astype(jnp.bfloat16)


def coarse_kernel(scalar_ref, prolong_ref, got_ref, ap_ref, out_ref, merged):
    merged[...] = jnp.zeros_like(merged)
    for s in range(KAP):
        total = got_ref[s].astype(jnp.float32)
        for peer in range(1, SIDE):
            total = total + got_ref[peer * KAP + s].astype(jnp.float32)
        ap = total.astype(jnp.bfloat16)
        ap_ref[s] = ap
        for k in range(KP):
            term = lax.dot_general(
                prolong_ref[k], ap, (((0,), (0,)), ((), ())), preferred_element_type=jnp.float32
            )
            bucket = scalar_ref[SPOT + k * KAP + s]
            merged[bucket] = merged[bucket] + term
    out_ref[...] = merged[...].astype(jnp.bfloat16)


def side_groups(even_along_x):
    groups = []
    for row in range(ROWS):
        along_x = (row % 2 == 0) == even_along_x
        for fixed in range(SIDE):
            groups.append(
                [
                    row * COLS + (move * SIDE + fixed if along_x else fixed * SIDE + move)
                    for move in range(SIDE)
                ]
            )
    return groups


def exchange_side(array, even_along_x):
    return lax.all_to_all(
        array,
        ("row", "col"),
        split_axis=0,
        concat_axis=0,
        tiled=True,
        axis_index_groups=side_groups(even_along_x),
    )


def from_neighbour(array):
    pairs = [
        (2 * z + core, 2 * ((z + (1 if core == 0 else -1)) % RINGS) + core)
        for z in range(RINGS)
        for core in range(2)
    ]
    return lax.ppermute(array, "row", pairs)


def to_sibling(array):
    return lax.ppermute(array, "row", [(r, r ^ 1) for r in range(ROWS)])


def gather_pieces(prolong, numbers):
    groups = [[2 * (low + 2 * k) + core for k in range(8)] for low in range(2) for core in range(2)]
    same8 = lax.all_gather(
        prolong.reshape(SHARD, TILE), "row", axis=0, tiled=True, axis_index_groups=groups
    )
    next8 = from_neighbour(same8)
    next8, numbers = lax.optimization_barrier((next8, numbers))
    own16 = jnp.concatenate([same8, next8])
    pieces = [own16, to_sibling(own16)]
    return [piece.reshape(-1, KP, TILE, TILE) for piece in pieces], numbers


def panel_place(tile_cols):
    row = lax.axis_index("row")
    ring = tile_cols // 2
    return (
        ring // 2
        + jnp.where((ring - row // 2) % 2 == 0, 0, 8)
        + jnp.where((tile_cols - row) % 2 == 0, 0, RINGS)
    )


def on_device(stiff_tiles, stiff_rows, stiff_cols, product_slot, prolong_tiles, coarse_dest):
    scalars = pl.BlockSpec(memory_space=pltpu.SMEM)
    vmem = pl.BlockSpec(memory_space=pltpu.VMEM)
    params = pltpu.CompilerParams(vmem_limit_bytes=24 * 2**20)
    prolong = prolong_tiles[0]
    numbers = jnp.concatenate(
        [
            panel_place(stiff_cols[0, 0]),
            stiff_rows[0, 0],
            product_slot[0, 0].reshape(KA * KP),
            coarse_dest.reshape(KP * KAP) % COARSE,
            jnp.full((1,), lax.axis_index("row") % 2, jnp.int32),
        ]
    )
    pieces, numbers = gather_pieces(prolong, numbers)
    sent = pl.pallas_call(
        product_kernel,
        out_shape=jax.ShapeDtypeStruct((COLS, BLOCK, TILE), jnp.bfloat16),
        in_specs=[scalars, vmem, vmem, vmem],
        out_specs=vmem,
        scratch_shapes=[
            pltpu.SMEM((KA,), jnp.int32),
            pltpu.SMEM((COLS,), jnp.int32),
        ],
        compiler_params=pltpu.CompilerParams(vmem_limit_bytes=K1_MIB * 2**20),
    )(numbers, stiff_tiles[0, 0], *pieces)
    got = exchange_side(sent, True)
    partial = pl.pallas_call(
        slot_kernel,
        out_shape=jax.ShapeDtypeStruct((SIDE * KAP, TILE, TILE), jnp.bfloat16),
        in_specs=[vmem],
        out_specs=vmem,
        scratch_shapes=[
            pltpu.VMEM((COLS, TILE), jnp.int32),
            pltpu.SMEM((COLS, TILE), jnp.int32),
            pltpu.VMEM((SIDE * KAP, TILE, TILE), jnp.float32),
            pltpu.SemaphoreType.DMA((1,)),
        ],
        compiler_params=params,
    )(got)
    summed = exchange_side(partial, False)
    ap, merged = pl.pallas_call(
        coarse_kernel,
        out_shape=(
            jax.ShapeDtypeStruct((KAP, TILE, TILE), jnp.bfloat16),
            jax.ShapeDtypeStruct((COARSE, TILE, TILE), jnp.bfloat16),
        ),
        in_specs=[scalars, vmem, vmem],
        out_specs=(vmem, vmem),
        scratch_shapes=[pltpu.VMEM((COARSE, TILE, TILE), jnp.float32)],
        compiler_params=params,
    )(numbers, prolong, summed)
    received = lax.all_to_all(merged, "col", split_axis=0, concat_axis=0, tiled=True)
    coarse = jnp.sum(received.reshape(COLS, CTD, TILE, TILE).astype(jnp.float32), axis=0)
    return (ap[None], coarse)


def solution(mesh):
    in_specs = (
        P("row", "col", None, None, None),
        P("row", "col", None),
        P("row", "col", None),
        P("row", "col", None, None),
        P(("row", "col"), None, None, None),
        P(("row", "col"), None, None),
    )
    out_specs = (P(("row", "col"), None, None, None), P(("row", "col"), None, None))
    return jax.shard_map(
        on_device, mesh=mesh, in_specs=in_specs, out_specs=out_specs, check_vma=False
    )
```

```python
import jax
import jax.numpy as jnp
from jax import lax
from jax.experimental import pallas as pl
from jax.experimental.pallas import tpu as pltpu
from jax.sharding import PartitionSpec as P

TILE = 128
KP = 3
KAP = 8
SIDE = 4
CTD = 2
COLS = 16
RINGS = 16
ROWS = 2 * RINGS
KA = 32
PAIR = KA // COLS
SHARD = KP * TILE
BODY = PAIR * SHARD
MARK = 16
BLOCK = BODY + MARK
COARSE = COLS * CTD
K1_MIB = 24
SPOT = 2 * KA + KA * KP


def product_kernel(scalar_ref, tile_ref, own_ref, other_ref, outs, order, count):
    for owner in range(COLS):
        count[owner] = 0
    for t in range(KA):
        owner = scalar_ref[KA + t]
        which = count[owner]
        count[owner] = which + 1
        order[owner * PAIR + which] = t
    lane = lax.broadcasted_iota(jnp.int32, (MARK, TILE), 1)
    flipped = scalar_ref[SPOT + KP * KAP]
    for place in range(COLS):
        owner = jnp.where(flipped == 0, place, place % SIDE * SIDE + place // SIDE)
        mark = jnp.zeros((MARK, TILE), jnp.float32)
        for which in range(PAIR):
            t = order[owner * PAIR + which]
            spot = scalar_ref[t]
            mine = spot < RINGS
            shard = spot % RINGS
            tile = tile_ref[t]
            for k in range(KP):
                q = which * KP + k
                block = jnp.where(mine, own_ref[shard, k], other_ref[shard, k])
                product = jnp.dot(tile, block, preferred_element_type=jnp.float32)
                outs[place, q * TILE : (q + 1) * TILE, :] = product.astype(jnp.bfloat16)
                value = scalar_ref[2 * KA + t * KP + k].astype(jnp.float32)
                mark = jnp.where(lane == q, value, mark)
        outs[place, BODY:, :] = mark.astype(jnp.bfloat16)


def slot_kernel(got_ref, out_ref, mark_int, mark_scalar, total, sem):
    marks = got_ref[:, BODY:, :].astype(jnp.float32)
    mark_int[...] = marks[:, 0, :].astype(jnp.int32)
    scalar_copy = pltpu.make_async_copy(mark_int, mark_scalar, sem.at[0])
    scalar_copy.start()
    total[...] = jnp.zeros_like(total)
    scalar_copy.wait()
    for peer in range(SIDE):
        for owner in range(SIDE):
            block = peer * SIDE + owner
            for q in range(PAIR * KP):
                where = owner * KAP + mark_scalar[block, q]
                part = got_ref[block, q * TILE : (q + 1) * TILE, :]
                total[where] = total[where] + part.astype(jnp.float32)
    out_ref[...] = total[...].astype(jnp.bfloat16)


def coarse_kernel(scalar_ref, prolong_ref, got_ref, ap_ref, out_ref, merged):
    merged[...] = jnp.zeros_like(merged)
    turned = [prolong_ref[k].astype(jnp.float32).T.astype(jnp.bfloat16) for k in range(KP)]
    for s in range(KAP):
        total = got_ref[s].astype(jnp.float32)
        for peer in range(1, SIDE):
            total = total + got_ref[peer * KAP + s].astype(jnp.float32)
        ap = total.astype(jnp.bfloat16)
        ap_ref[s] = ap
        for k in range(KP):
            term = jnp.dot(turned[k], ap, preferred_element_type=jnp.float32)
            bucket = scalar_ref[SPOT + k * KAP + s]
            merged[bucket] = merged[bucket] + term
    out_ref[...] = merged[...].astype(jnp.bfloat16)


def side_groups(even_along_x):
    groups = []
    for row in range(ROWS):
        along_x = (row % 2 == 0) == even_along_x
        for fixed in range(SIDE):
            groups.append(
                [
                    row * COLS + (move * SIDE + fixed if along_x else fixed * SIDE + move)
                    for move in range(SIDE)
                ]
            )
    return groups


def exchange_side(array, even_along_x):
    return lax.all_to_all(
        array,
        ("row", "col"),
        split_axis=0,
        concat_axis=0,
        tiled=True,
        axis_index_groups=side_groups(even_along_x),
    )


def from_neighbour(array):
    pairs = [
        (2 * z + core, 2 * ((z + (1 if core == 0 else -1)) % RINGS) + core)
        for z in range(RINGS)
        for core in range(2)
    ]
    return lax.ppermute(array, "row", pairs)


def to_sibling(array):
    return lax.ppermute(array, "row", [(r, r ^ 1) for r in range(ROWS)])


def gather_pieces(prolong, numbers):
    groups = [[2 * (low + 2 * k) + core for k in range(8)] for low in range(2) for core in range(2)]
    same8 = lax.all_gather(
        prolong.reshape(SHARD, TILE), "row", axis=0, tiled=True, axis_index_groups=groups
    )
    next8 = from_neighbour(same8)
    next8, numbers = lax.optimization_barrier((next8, numbers))
    own16 = jnp.concatenate([same8, next8])
    pieces = [own16, to_sibling(own16)]
    return [piece.reshape(-1, KP, TILE, TILE) for piece in pieces], numbers


def panel_place(tile_cols):
    row = lax.axis_index("row")
    ring = tile_cols // 2
    return (
        ring // 2
        + jnp.where((ring - row // 2) % 2 == 0, 0, 8)
        + jnp.where((tile_cols - row) % 2 == 0, 0, RINGS)
    )


def on_device(stiff_tiles, stiff_rows, stiff_cols, product_slot, prolong_tiles, coarse_dest):
    scalars = pl.BlockSpec(memory_space=pltpu.SMEM)
    vmem = pl.BlockSpec(memory_space=pltpu.VMEM)
    params = pltpu.CompilerParams(vmem_limit_bytes=24 * 2**20)
    prolong = prolong_tiles[0]
    numbers = jnp.concatenate(
        [
            panel_place(stiff_cols[0, 0]),
            stiff_rows[0, 0],
            product_slot[0, 0].reshape(KA * KP),
            coarse_dest.reshape(KP * KAP) % COARSE,
            jnp.full((1,), lax.axis_index("row") % 2, jnp.int32),
        ]
    )
    pieces, numbers = gather_pieces(prolong, numbers)
    sent = pl.pallas_call(
        product_kernel,
        out_shape=jax.ShapeDtypeStruct((COLS, BLOCK, TILE), jnp.bfloat16),
        in_specs=[scalars, vmem, vmem, vmem],
        out_specs=vmem,
        scratch_shapes=[
            pltpu.SMEM((KA,), jnp.int32),
            pltpu.SMEM((COLS,), jnp.int32),
        ],
        compiler_params=pltpu.CompilerParams(vmem_limit_bytes=K1_MIB * 2**20),
    )(numbers, stiff_tiles[0, 0], *pieces)
    got = exchange_side(sent, True)
    partial = pl.pallas_call(
        slot_kernel,
        out_shape=jax.ShapeDtypeStruct((SIDE * KAP, TILE, TILE), jnp.bfloat16),
        in_specs=[vmem],
        out_specs=vmem,
        scratch_shapes=[
            pltpu.VMEM((COLS, TILE), jnp.int32),
            pltpu.SMEM((COLS, TILE), jnp.int32),
            pltpu.VMEM((SIDE * KAP, TILE, TILE), jnp.float32),
            pltpu.SemaphoreType.DMA((1,)),
        ],
        compiler_params=params,
    )(got)
    summed = exchange_side(partial, False)
    ap, merged = pl.pallas_call(
        coarse_kernel,
        out_shape=(
            jax.ShapeDtypeStruct((KAP, TILE, TILE), jnp.bfloat16),
            jax.ShapeDtypeStruct((COARSE, TILE, TILE), jnp.bfloat16),
        ),
        in_specs=[scalars, vmem, vmem],
        out_specs=(vmem, vmem),
        scratch_shapes=[pltpu.VMEM((COARSE, TILE, TILE), jnp.float32)],
        compiler_params=params,
    )(numbers, prolong, summed)
    received = lax.all_to_all(merged, "col", split_axis=0, concat_axis=0, tiled=True)
    coarse = jnp.sum(received.reshape(COLS, CTD, TILE, TILE).astype(jnp.float32), axis=0)
    return (ap[None], coarse)


def solution(mesh):
    in_specs = (
        P("row", "col", None, None, None),
        P("row", "col", None),
        P("row", "col", None),
        P("row", "col", None, None),
        P(("row", "col"), None, None, None),
        P(("row", "col"), None, None),
    )
    out_specs = (P(("row", "col"), None, None, None), P(("row", "col"), None, None))
    return jax.shard_map(
        on_device, mesh=mesh, in_specs=in_specs, out_specs=out_specs, check_vma=False
    )
```

```python
import jax
import jax.numpy as jnp
from jax import lax
from jax.experimental import pallas as pl
from jax.experimental.pallas import tpu as pltpu
from jax.sharding import PartitionSpec as P

TILE = 128
KP = 3
KAP = 8
SIDE = 4
CTD = 2
COLS = 16
RINGS = 16
ROWS = 2 * RINGS
KA = 32
PAIR = KA // COLS
SHARD = KP * TILE
BODY = PAIR * SHARD
MARK = 16
BLOCK = BODY + MARK
COARSE = COLS * CTD
K1_MIB = 24
SPOT = 2 * KA + KA * KP


def product_kernel(scalar_ref, tile_ref, own_ref, other_ref, outs, order, count):
    for owner in range(COLS):
        count[owner] = 0
    for t in range(KA):
        owner = scalar_ref[KA + t]
        which = count[owner]
        count[owner] = which + 1
        order[owner * PAIR + which] = t
    lane = lax.broadcasted_iota(jnp.int32, (MARK, TILE), 1)
    flipped = scalar_ref[SPOT + KP * KAP]
    for place in range(COLS):
        owner = jnp.where(flipped == 0, place, place % SIDE * SIDE + place // SIDE)
        mark = jnp.zeros((MARK, TILE), jnp.float32)
        for which in range(PAIR):
            t = order[owner * PAIR + which]
            spot = scalar_ref[t]
            mine = spot < RINGS
            shard = spot % RINGS
            tile = tile_ref[t]
            for k in range(KP):
                q = which * KP + k
                block = jnp.where(mine, own_ref[shard, k], other_ref[shard, k])
                product = jnp.dot(tile, block, preferred_element_type=jnp.float32)
                outs[place, q * TILE : (q + 1) * TILE, :] = product.astype(jnp.bfloat16)
                value = scalar_ref[2 * KA + t * KP + k].astype(jnp.float32)
                mark = jnp.where(lane == q, value, mark)
        outs[place, BODY:, :] = mark.astype(jnp.bfloat16)


def slot_kernel(got_ref, out_ref, mark_int, mark_scalar, total, sem):
    marks = got_ref[:, BODY:, :].astype(jnp.float32)
    mark_int[...] = marks[:, 0, :].astype(jnp.int32)
    scalar_copy = pltpu.make_async_copy(mark_int, mark_scalar, sem.at[0])
    scalar_copy.start()
    total[...] = jnp.zeros_like(total)
    scalar_copy.wait()
    for owner in range(SIDE):
        for peer in range(SIDE):
            block = peer * SIDE + owner
            for q in range(PAIR * KP):
                where = owner * KAP + mark_scalar[block, q]
                part = got_ref[block, q * TILE : (q + 1) * TILE, :]
                total[where] = total[where] + part.astype(jnp.float32)
        mine = slice(owner * KAP, (owner + 1) * KAP)
        out_ref[mine] = total[mine].astype(jnp.bfloat16)


def coarse_kernel(scalar_ref, prolong_ref, got_ref, ap_ref, out_ref, merged):
    merged[...] = jnp.zeros_like(merged)
    turned = [prolong_ref[k].astype(jnp.float32).T.astype(jnp.bfloat16) for k in range(KP)]
    for s in range(KAP):
        total = got_ref[s].astype(jnp.float32)
        for peer in range(1, SIDE):
            total = total + got_ref[peer * KAP + s].astype(jnp.float32)
        ap = total.astype(jnp.bfloat16)
        ap_ref[s] = ap
        for k in range(KP):
            term = jnp.dot(turned[k], ap, preferred_element_type=jnp.float32)
            bucket = scalar_ref[SPOT + k * KAP + s]
            merged[bucket] = merged[bucket] + term
    out_ref[...] = merged[...].astype(jnp.bfloat16)


def side_groups(even_along_x):
    groups = []
    for row in range(ROWS):
        along_x = (row % 2 == 0) == even_along_x
        for fixed in range(SIDE):
            groups.append(
                [
                    row * COLS + (move * SIDE + fixed if along_x else fixed * SIDE + move)
                    for move in range(SIDE)
                ]
            )
    return groups


def exchange_side(array, even_along_x):
    return lax.all_to_all(
        array,
        ("row", "col"),
        split_axis=0,
        concat_axis=0,
        tiled=True,
        axis_index_groups=side_groups(even_along_x),
    )


def from_neighbour(array):
    pairs = [
        (2 * z + core, 2 * ((z + (1 if core == 0 else -1)) % RINGS) + core)
        for z in range(RINGS)
        for core in range(2)
    ]
    return lax.ppermute(array, "row", pairs)


def to_sibling(array):
    return lax.ppermute(array, "row", [(r, r ^ 1) for r in range(ROWS)])


def gather_pieces(prolong, numbers):
    groups = [[2 * (low + 2 * k) + core for k in range(8)] for low in range(2) for core in range(2)]
    same8 = lax.all_gather(
        prolong.reshape(SHARD, TILE), "row", axis=0, tiled=True, axis_index_groups=groups
    )
    next8 = from_neighbour(same8)
    next8, numbers = lax.optimization_barrier((next8, numbers))
    own16 = jnp.concatenate([same8, next8])
    pieces = [own16, to_sibling(own16)]
    return [piece.reshape(-1, KP, TILE, TILE) for piece in pieces], numbers


def panel_place(tile_cols):
    row = lax.axis_index("row")
    ring = tile_cols // 2
    return (
        ring // 2
        + jnp.where((ring - row // 2) % 2 == 0, 0, 8)
        + jnp.where((tile_cols - row) % 2 == 0, 0, RINGS)
    )


def on_device(stiff_tiles, stiff_rows, stiff_cols, product_slot, prolong_tiles, coarse_dest):
    scalars = pl.BlockSpec(memory_space=pltpu.SMEM)
    vmem = pl.BlockSpec(memory_space=pltpu.VMEM)
    params = pltpu.CompilerParams(vmem_limit_bytes=24 * 2**20)
    prolong = prolong_tiles[0]
    numbers = jnp.concatenate(
        [
            panel_place(stiff_cols[0, 0]),
            stiff_rows[0, 0],
            product_slot[0, 0].reshape(KA * KP),
            coarse_dest.reshape(KP * KAP) % COARSE,
            jnp.full((1,), lax.axis_index("row") % 2, jnp.int32),
        ]
    )
    pieces, numbers = gather_pieces(prolong, numbers)
    sent = pl.pallas_call(
        product_kernel,
        out_shape=jax.ShapeDtypeStruct((COLS, BLOCK, TILE), jnp.bfloat16),
        in_specs=[scalars, vmem, vmem, vmem],
        out_specs=vmem,
        scratch_shapes=[
            pltpu.SMEM((KA,), jnp.int32),
            pltpu.SMEM((COLS,), jnp.int32),
        ],
        compiler_params=pltpu.CompilerParams(vmem_limit_bytes=K1_MIB * 2**20),
    )(numbers, stiff_tiles[0, 0], *pieces)
    got = exchange_side(sent, True)
    partial = pl.pallas_call(
        slot_kernel,
        out_shape=jax.ShapeDtypeStruct((SIDE * KAP, TILE, TILE), jnp.bfloat16),
        in_specs=[vmem],
        out_specs=vmem,
        scratch_shapes=[
            pltpu.VMEM((COLS, TILE), jnp.int32),
            pltpu.SMEM((COLS, TILE), jnp.int32),
            pltpu.VMEM((SIDE * KAP, TILE, TILE), jnp.float32),
            pltpu.SemaphoreType.DMA((1,)),
        ],
        compiler_params=params,
    )(got)
    summed = exchange_side(partial, False)
    ap, merged = pl.pallas_call(
        coarse_kernel,
        out_shape=(
            jax.ShapeDtypeStruct((KAP, TILE, TILE), jnp.bfloat16),
            jax.ShapeDtypeStruct((COARSE, TILE, TILE), jnp.bfloat16),
        ),
        in_specs=[scalars, vmem, vmem],
        out_specs=(vmem, vmem),
        scratch_shapes=[pltpu.VMEM((COARSE, TILE, TILE), jnp.float32)],
        compiler_params=params,
    )(numbers, prolong, summed)
    received = lax.all_to_all(merged, "col", split_axis=0, concat_axis=0, tiled=True)
    coarse = jnp.sum(received.reshape(COLS, CTD, TILE, TILE).astype(jnp.float32), axis=0)
    return (ap[None], coarse)


def solution(mesh):
    in_specs = (
        P("row", "col", None, None, None),
        P("row", "col", None),
        P("row", "col", None),
        P("row", "col", None, None),
        P(("row", "col"), None, None, None),
        P(("row", "col"), None, None),
    )
    out_specs = (P(("row", "col"), None, None, None), P(("row", "col"), None, None))
    return jax.shard_map(
        on_device, mesh=mesh, in_specs=in_specs, out_specs=out_specs, check_vma=False
    )
```
